32 devices in a mesh: seq: 8 (over z, x), vocab: 4 (over y, core).
Axes of the slice: x: 2, y: 2, z: 4, core: 2. Of those that a mesh axis runs over, the one named last changes fastest.
Arguments:
- hidden: bfloat16 [512, 4096], P('seq'), may hold values from -12 to 12
- head_weight: bfloat16 [4096, 126464], P(None, ('seq', 'vocab')), may hold values from -3 to 3
- teacher: bfloat16 [64, 126464], P(None, ('seq', 'vocab')), may hold values from -320 to 320
- positions: int32 [8, 8], P('seq'), may hold values from 0 to 63, as said below
- counts: int32 [8], P('seq'), may hold values from 1 to 8, 32 in all
Outputs:
- grad_hidden: bfloat16 [64, 4096], P(('seq', 'vocab'))
- grad_head: bfloat16 [4096, 126464], P(None, ('seq', 'vocab'))
The draws below stay inside these ranges and needn't reach their ends.
Inputs may be any that keep to these rules, and one draw needn't show every extreme that they name: Each row holds 8 distinct token positions within its seq shard's block of 64 tokens; the first counts[s] of row s are its masked tokens. The counts sum to exactly 32.
All inputs are finite; a program needn't handle non-finite values. No bound on the sum of `counts` on one device may be relied on, other than what follows from the above.
Results may differ from the reference program's by a relative error of at most 0.012.
Values may be sent and summed in bfloat16 or wider, within the bound.
A program may use at most 128 MiB of HBM per device.

```python
import math
import jax
import jax.numpy as jnp
import numpy as np
from jax import lax

D = 4096
VOCAB = 126464
TOK_DEV = 64
SPAN = 1
CAP = 8
TOKENS = 512
SEQS = 8
SLOTS = 64
MASKED = 32
N_SEQ = 8


def draw_hidden(key, part):
    key = jax.random.fold_in(key, 11)
    k_body, k_scale = jax.random.split(key, 2)
    row_scale = jnp.exp(jax.random.uniform(k_scale, (TOKENS, 1), minval=math.log(0.02), maxval=math.log(0.2)))
    values = jax.random.normal(k_body, (TOKENS, D)) * row_scale
    return jnp.clip(values, -12.0, 12.0).astype(jnp.bfloat16)


def draw_head_weight(key, part):
    key = jax.random.fold_in(key, 12)
    k_body, k_scale = jax.random.split(key, 2)
    col_scale = jnp.exp(jax.random.uniform(k_scale, (1, VOCAB), minval=math.log(0.9), maxval=math.log(9.0)))
    values = jax.random.normal(k_body, (D, VOCAB)) * col_scale / math.sqrt(D)
    return jnp.clip(values, -3.0, 3.0).astype(jnp.bfloat16)


def draw_teacher(key, part):
    key = jax.random.fold_in(key, 13)
    k_body, k_row, k_col = jax.random.split(key, 3)
    row_scale = jnp.exp(jax.random.uniform(k_row, (SLOTS, 1), minval=math.log(0.02), maxval=math.log(0.2)))
    col_scale = jnp.exp(jax.random.uniform(k_col, (1, VOCAB), minval=math.log(0.9), maxval=math.log(9.0)))
    values = jax.random.normal(k_body, (SLOTS, VOCAB)) * row_scale * col_scale
    return jnp.clip(values, -320.0, 320.0).astype(jnp.bfloat16)


def draw_positions(key, part):
    key = jax.random.fold_in(key, 14)
    shard_count = TOKENS // TOK_DEV
    column = jnp.arange(TOK_DEV, dtype=jnp.int32)[None, :]
    row = jnp.arange(shard_count, dtype=jnp.int32)[:, None]
    scores = jax.random.randint(key, (shard_count, TOK_DEV), 0, 1 << 20) * TOK_DEV + column
    forced = (row == 0) & ((column == 0) | (column == TOK_DEV - 1))
    scores = jnp.where(forced, (1 << 21) * TOK_DEV + column, scores)
    unused, chosen = lax.top_k(scores, CAP)
    return chosen.astype(jnp.int32)


def length_profile(count, total, limit, lean):
    loads = [(1 << 20) // math.isqrt(standing ** lean) + 1 for standing in range(2, count + 1)]
    surplus, given = total - limit - (count - 1), [1] * (count - 1)
    while surplus > 0:
        movable = [i for i in range(count - 1) if given[i] < limit]
        mass, budget = sum([loads[i] for i in movable]), surplus
        for i in movable:
            extra = min(limit - given[i], max(1, budget * loads[i] // mass), surplus)
            given[i] = given[i] + extra
            surplus = surplus - extra
    return np.array([limit] + given)


def uneven_parts(stream_key, number_of, total, bound, slope):
    if number_of == 2:
        one = jax.random.randint(stream_key, (), max(1, total - bound), min(bound, total - 1) + 1)
        return jnp.stack([one, total - one])
    lengths = jnp.asarray(length_profile(number_of, total, bound, slope), jnp.int32)
    twos = (number_of - 1) // 2
    donor, receiver = lengths[1:1 + 2 * twos:2], lengths[2:2 + 2 * twos:2]
    margin = jnp.minimum(donor - 1, bound - receiver)
    shifted = jax.random.randint(jax.random.fold_in(stream_key, 1), (twos,), 0, 1 << 20) % (margin + 1)
    lengths = lengths.at[1:1 + 2 * twos:2].set(donor - shifted).at[2:2 + 2 * twos:2].set(receiver + shifted)
    return lengths[jax.random.permutation(jax.random.fold_in(stream_key, 2), number_of)]


def setup_inputs(seed: int = 0) -> dict:
    splits = jax.random.split(jax.random.key(seed), 6)
    hidden = draw_hidden(jax.random.fold_in(splits[5], 71), 0)
    head_weight = draw_head_weight(jax.random.fold_in(splits[5], 71), 0)
    teacher = draw_teacher(jax.random.fold_in(splits[5], 71), 0)
    positions = draw_positions(jax.random.fold_in(splits[5], 71), 0)
    counts = uneven_parts(splits[4], N_SEQ, MASKED, CAP, 2).astype(jnp.int32)
    return dict(hidden=hidden, head_weight=head_weight, teacher=teacher, positions=positions, counts=counts)


loss_scale = 1024.0


def reference(hidden, head_weight, teacher, positions, counts):
    offsets = (jnp.arange(N_SEQ, dtype=jnp.int32) * TOK_DEV)[:, None]
    rows_index = (positions + offsets).reshape(-1).astype(jnp.int32)
    picked = jnp.take(hidden, rows_index, axis=0)
    seq_count = jnp.sum(counts.reshape(SEQS, SPAN), axis=1).astype(jnp.int32)
    per_slot = jnp.repeat(seq_count, SPAN * CAP)
    slot_rank = jnp.arange(CAP, dtype=jnp.int32)[None, :]
    validity = (slot_rank < counts[:, None]).reshape(-1)
    weight = jnp.where(validity, loss_scale / per_slot.astype(jnp.float32), 0.0)
    student = jnp.dot(picked, head_weight, preferred_element_type=jnp.float32)
    prob_student = jax.nn.softmax(student, axis=-1)
    prob_teacher = jax.nn.softmax(teacher.astype(jnp.float32), axis=-1)
    grad_logits = (weight[:, None] * (prob_student - prob_teacher)).astype(jnp.bfloat16)
    grad_head = lax.dot_general(picked, grad_logits, (((0,), (0,)), ((), ())), preferred_element_type=jnp.float32).astype(jnp.bfloat16)
    grad_hidden = lax.dot_general(grad_logits, head_weight, (((1,), (1,)), ((), ())), preferred_element_type=jnp.float32).astype(jnp.bfloat16)
    return grad_hidden, grad_head
```

```python
import functools

import jax
import jax.numpy as jnp
from jax import lax
from jax.experimental import pallas as pl
from jax.experimental.pallas import tpu as pltpu
from jax.sharding import PartitionSpec as P

MESH = pl.DeviceIdType.MESH
LOSS_SCALE = 1024.0
F32 = jnp.float32
BF16 = jnp.bfloat16


def chunks_of(size, step):
    if size % 16:
        return 0, 0, size
    full = size // step
    return full, full * step, size - full * step


def front_kernel(
    n_seq, n_voc, step,
    pos_ref, cnt_ref, hid_ref, tea_ref, w_hbm,
    picked_ref, grad_ref, gh_ref,
    w_ref, gb, picked, stu, tex, grad, st1, st2, xs, xr, bs, br, cg, gh32,
    w_sem, g1s, g1r, g2s, g2r, s1s, s1r, s2s, s2r, as_, ar, bss, bsr, cs, cr,
):
    slots, vocab = tea_ref.shape
    depth = hid_ref.shape[1]
    cap = pos_ref.shape[1]
    half = depth // 2
    quart = depth // 4
    own_cols = depth // n_voc
    sub = own_cols // 2
    halves = n_voc // 2
    group = n_seq * halves
    lanes = st1.shape[2]
    s = lax.axis_index("seq")
    v = lax.axis_index("vocab")
    core = v % 2
    other = 1 - core
    pair = v + 1 - 2 * core
    hv = v // 2
    flat = s * halves + hv
    full, tail_at, tail = chunks_of(vocab, step)

    def w_copy(i):
        rows = pl.ds(pl.multiple_of(i * step, step), step)
        return pltpu.make_async_copy(w_hbm.at[rows], w_ref.at[rows], w_sem.at[i])

    def w_tail():
        if full == 0:
            return pltpu.make_async_copy(w_hbm, w_ref, w_sem.at[0])
        rows = pl.ds(tail_at, tail)
        return pltpu.make_async_copy(w_hbm.at[rows], w_ref.at[rows], w_sem.at[full])

    if full:
        @pl.loop(0, full)
        def _(i):
            w_copy(i).start()
    if tail:
        w_tail().start()

    barrier = pltpu.get_barrier_semaphore()

    @pl.loop(1, group)
    def _(k):
        to = (flat + k) % group
        pl.semaphore_signal(
            barrier, inc=1, device_id=(to // halves, 2 * (to % halves) + core), device_id_type=MESH
        )

    @pl.loop(0, halves)
    def _(k):
        pl.semaphore_signal(barrier, inc=1, device_id=(s, 2 * k + other), device_id_type=MESH)

    tokens = hid_ref.shape[0]
    at_row = lax.broadcasted_iota(jnp.int32, (cap, tokens), 0)
    at_tok = lax.broadcasted_iota(jnp.int32, (cap, tokens), 1)
    hot = jnp.zeros((cap, tokens), F32)
    for k in range(cap):
        hot = jnp.where((at_row == k) & (at_tok == pos_ref[0, k]), 1.0, hot)
    mine = jnp.dot(hot.astype(BF16), hid_ref[...], preferred_element_type=F32)
    for h in range(2):
        lo = mine[:, h * half : h * half + quart]
        hi = mine[:, h * half + quart : (h + 1) * half]
        gb[s, h] = jnp.concatenate([lo, hi], axis=0).astype(BF16)

    pl.semaphore_wait(barrier, group - 1 + halves)

    def gather1(k, frm):
        return pltpu.make_async_remote_copy(
            src_ref=gb.at[frm, core], dst_ref=gb.at[frm, core],
            send_sem=g1s.at[k], recv_sem=g1r.at[frm],
            device_id=((s + k) % n_seq, v), device_id_type=MESH,
        )

    def gather2(frm, col):
        return pltpu.make_async_remote_copy(
            src_ref=gb.at[frm, col], dst_ref=gb.at[frm, col],
            send_sem=g2s.at[frm], recv_sem=g2r.at[frm],
            device_id=(s, pair), device_id_type=MESH,
        )

    @pl.loop(1, n_seq)
    def _(k):
        gather1(k, s).start()

    def over(body, init):
        carry = init
        if full:
            carry = lax.fori_loop(
                0, full, lambda i, c: body(pl.ds(pl.multiple_of(i * step, step), step), c), carry
            )
        if tail:
            carry = body(pl.ds(tail_at, tail), carry)
        return carry

    low = jnp.full((slots, 1), -jnp.inf, F32)
    none = jnp.zeros((slots, 1), F32)
    top_t = over(
        lambda at, c: jnp.maximum(c, jnp.max(tea_ref[:, at].astype(F32), axis=1, keepdims=True)), low
    )

    def teacher_total(at, c):
        e = jnp.exp(tea_ref[:, at].astype(F32) - top_t)
        tex[:, at] = e
        return c + jnp.sum(e, axis=1, keepdims=True)

    tot_t = over(teacher_total, none)

    @pl.loop(1, n_seq)
    def _(k):
        frm = (s + n_seq - k) % n_seq
        gather1(k, frm).wait_recv()
        gather2(frm, core).start()

    @pl.loop(1, n_seq)
    def _(k):
        gather2((s + n_seq - k) % n_seq, other).wait_recv()

    @pl.loop(0, n_seq // 2)
    def _(i):
        rows = pl.ds(pl.multiple_of(i * 2 * cap, 2 * cap), 2 * cap)
        for h in range(2):
            a = gb[2 * i, h].astype(F32)
            b = gb[2 * i + 1, h].astype(F32)
            for j in range(2):
                both = jnp.concatenate([a[j * cap : (j + 1) * cap], b[j * cap : (j + 1) * cap]], axis=0)
                picked[rows, h * half + j * quart : h * half + (j + 1) * quart] = both.astype(BF16)

    picked_ref[...] = picked[...]

    def student(at, top):
        block = lax.dot_general(
            w_ref[at, :], picked[...], (((1,), (1,)), ((), ())), preferred_element_type=F32
        )
        block = block.T
        stu[:, at] = block
        return jnp.maximum(top, jnp.max(block, axis=1, keepdims=True))

    top_s = low
    if full:
        def student_step(i, top):
            w_copy(i).wait()
            return student(pl.ds(pl.multiple_of(i * step, step), step), top)

        top_s = lax.fori_loop(0, full, student_step, top_s)
    if tail:
        w_tail().wait()
        top_s = student(pl.ds(tail_at, tail), top_s)

    def student_total(at, c):
        e = jnp.exp(stu[:, at] - top_s)
        stu[:, at] = e
        return c + jnp.sum(e, axis=1, keepdims=True)

    tot_s = over(student_total, none)

    lane = lax.broadcasted_iota(jnp.int32, (slots, 128), 1)
    wide = jnp.where(lane == 0, top_s, jnp.where(lane == 1, tot_s, jnp.where(lane == 2, top_t, tot_t)))
    if lanes > slots:
        wide = jnp.concatenate([wide, jnp.zeros((lanes - slots, 128), F32)], axis=0)
    st1[v] = wide.T[0:8, :]

    def stats1(k, frm):
        return pltpu.make_async_remote_copy(
            src_ref=st1.at[frm], dst_ref=st1.at[frm],
            send_sem=s1s.at[k], recv_sem=s1r.at[frm],
            device_id=(s, (v + k) % n_voc), device_id_type=MESH,
        )

    def stats2(k, frm):
        return pltpu.make_async_remote_copy(
            src_ref=st2.at[frm], dst_ref=st2.at[frm],
            send_sem=s2s.at[k], recv_sem=s2r.at[frm],
            device_id=((s + k) % n_seq, v), device_id_type=MESH,
        )

    def merge(ref):
        x = ref[...]
        ms, zs, mt, zt = x[:, 0:1, :], x[:, 1:2, :], x[:, 2:3, :], x[:, 3:4, :]
        top1 = jnp.max(ms, axis=0)
        top2 = jnp.max(mt, axis=0)
        return (
            top1, jnp.sum(zs * jnp.exp(ms - top1[None]), axis=0),
            top2, jnp.sum(zt * jnp.exp(mt - top2[None]), axis=0),
            jnp.sum(x[:, 4:5, :], axis=0),
        )

    for k in range(1, n_voc):
        stats1(k, v).start()
    for k in range(1, n_voc):
        stats1(k, (v + n_voc - k) % n_voc).wait_recv()
    slot_lane = lax.broadcasted_iota(jnp.int32, (1, lanes), 1)
    count = cnt_ref[0].astype(F32)
    my_count = jnp.where(slot_lane // cap == s, count, 0.0)
    m1, z1, m2, z2, _ = merge(st1)
    st2[s] = jnp.concatenate([m1, z1, m2, z2, my_count, jnp.zeros((3, lanes), F32)], axis=0)

    @pl.loop(1, n_seq)
    def _(k):
        stats2(k, s).start()

    @pl.loop(1, n_seq)
    def _(k):
        stats2(k, (s + n_seq - k) % n_seq).wait_recv()

    m1, z1, m2, z2, counts = merge(st2)
    weight = jnp.where(
        (slot_lane % cap).astype(F32) < counts, LOSS_SCALE / jnp.maximum(counts, 1.0), 0.0
    )
    rows = jnp.concatenate([m1, weight / z1, m2, weight / z2, jnp.zeros((124, lanes), F32)], axis=0)
    cols = rows.T[0:slots]
    scale_s = cols[:, 1:2] * jnp.exp(top_s - cols[:, 0:1])
    scale_t = cols[:, 3:4] * jnp.exp(top_t - cols[:, 2:3])

    def logits(at, c):
        grad[:, at] = (scale_s * stu[:, at] - scale_t * tex[:, at]).astype(BF16)
        return c

    over(logits, 0)
    grad_ref[...] = grad[...]

    def part(q, store):
        @pl.loop(0, 2)
        def _(j):
            at = pl.ds(pl.multiple_of(q * own_cols + j * sub, sub), sub)
            store(j, jnp.dot(grad[...], w_ref[:, at], preferred_element_type=F32))

    def to_pair(i):
        return pltpu.make_async_remote_copy(
            src_ref=xs.at[i], dst_ref=xr.at[i], send_sem=as_.at[i], recv_sem=ar.at[i],
            device_id=(s, pair), device_id_type=MESH,
        )

    def to_owner(i, k):
        h = (hv + 1 + i) % halves
        seq = (s + k) % n_seq
        return pltpu.make_async_remote_copy(
            src_ref=bs.at[i, seq], dst_ref=br.at[flat],
            send_sem=bss.at[i, k], recv_sem=bsr.at[flat],
            device_id=(seq, 2 * h + core), device_id_type=MESH,
        )

    for i in range(halves):
        h = (hv + 1 + i) % halves

        def store_pair(j, value, i=i):
            xs[i, j] = value

        part(2 * h + other, store_pair)
        to_pair(i).start()

        def store_own(j, value, i=i):
            for q in range(n_seq):
                bs32 = value[q * cap : (q + 1) * cap]
                gh32[q, pl.ds(pl.multiple_of(j * cap, cap), cap), :] = bs32

        part(2 * h + core, store_own)
        to_pair(i).wait_recv()
        for q in range(n_seq):
            for_q = [xr[i, j, q * cap : (q + 1) * cap, :] for j in range(2)]
            bs[i, q] = (gh32[q] + jnp.concatenate(for_q, axis=0)).astype(BF16)
        last = i == halves - 1
        for k in range(1 if last else 0, n_seq):
            to_owner(i, k).start()

    br[flat] = bs[halves - 1, s]

    def got(k):
        frm = (flat + k) % group
        return pltpu.make_async_remote_copy(
            src_ref=bs.at[0, 0], dst_ref=br.at[frm],
            send_sem=bss.at[0, 0], recv_sem=bsr.at[frm],
            device_id=(frm // halves, 2 * (frm % halves) + core), device_id_type=MESH,
        )

    @pl.loop(1, group)
    def _(k):
        got(k).wait_recv()

    total = lax.fori_loop(
        0, group, lambda k, c: c + br[k].astype(F32), jnp.zeros((2 * cap, sub), F32)
    )
    cg[v] = total.astype(BF16)

    def to_row(k, frm):
        return pltpu.make_async_remote_copy(
            src_ref=cg.at[frm], dst_ref=cg.at[frm], send_sem=cs.at[k], recv_sem=cr.at[frm],
            device_id=(s, (v + k) % n_voc), device_id_type=MESH,
        )

    for k in range(1, n_voc):
        to_row(k, v).start()
    for k in range(1, n_voc):
        to_row(k, (v + n_voc - k) % n_voc).wait_recv()
    per = cap // n_voc
    row_at = lax.broadcasted_iota(jnp.int32, (cap, sub), 0)
    for r in range(per):
        for q in range(n_voc):
            both = cg[q].astype(F32)
            for j in range(2):
                row = jnp.sum(
                    jnp.where(row_at == per * v + r, both[j * cap : (j + 1) * cap], 0.0),
                    axis=0, keepdims=True,
                )
                gh_ref[r : r + 1, q * own_cols + j * sub : q * own_cols + (j + 1) * sub] = row

    @pl.loop(1, n_seq)
    def _(k):
        gather1(k, s).wait_send()
        gather2((s + n_seq - k) % n_seq, core).wait_send()
        stats2(k, s).wait_send()

    for k in range(1, n_voc):
        stats1(k, v).wait_send()
        to_row(k, v).wait_send()
    for i in range(halves):
        to_pair(i).wait_send()
        for k in range(1 if i == halves - 1 else 0, n_seq):
            to_owner(i, k).wait_send()


def head_kernel(g_ref, p_ref, out_ref):
    out_ref[...] = lax.dot_general(
        g_ref[...], p_ref[...], (((0,), (0,)), ((), ())), preferred_element_type=F32
    ).astype(BF16)


def per_device(n_seq, n_voc, hidden, head_weight, teacher, positions, counts):
    slots, vocab = teacher.shape
    depth = hidden.shape[1]
    cap = positions.shape[1]
    halves = n_voc // 2
    group = n_seq * halves
    sub = depth // n_voc // 2
    lanes = -(-slots // 128) * 128
    step = 512
    n_chunks = chunks_of(vocab, step)[0] + 1
    vmem = pl.BlockSpec(memory_space=pltpu.VMEM)
    smem = pl.BlockSpec(memory_space=pltpu.SMEM)
    dma = pltpu.SemaphoreType.DMA
    picked, grad, gh = pl.pallas_call(
        functools.partial(front_kernel, n_seq, n_voc, step),
        out_shape=(
            jax.ShapeDtypeStruct((slots, depth), BF16),
            jax.ShapeDtypeStruct((slots, vocab), BF16),
            jax.ShapeDtypeStruct((cap // n_voc, depth), F32),
        ),
        in_specs=[smem, smem, vmem, vmem, pl.BlockSpec(memory_space=pl.ANY)],
        out_specs=(vmem, vmem, vmem),
        scratch_shapes=[
            pltpu.VMEM((vocab, depth), BF16),
            pltpu.VMEM((n_seq, 2, 2 * cap, depth // 4), BF16),
            pltpu.VMEM((slots, depth), BF16),
            pltpu.VMEM((slots, vocab), F32),
            pltpu.VMEM((slots, vocab), F32),
            pltpu.VMEM((slots, vocab), BF16),
            pltpu.VMEM((n_voc, 8, lanes), F32),
            pltpu.VMEM((n_seq, 8, lanes), F32),
            pltpu.VMEM((halves, 2, slots, sub), F32),
            pltpu.VMEM((halves, 2, slots, sub), F32),
            pltpu.VMEM((halves, n_seq, 2 * cap, sub), BF16),
            pltpu.VMEM((group, 2 * cap, sub), BF16),
            pltpu.VMEM((n_voc, 2 * cap, sub), BF16),
            pltpu.VMEM((n_seq, 2 * cap, sub), F32),
            dma((n_chunks,)),
            dma((n_seq,)), dma((n_seq,)), dma((n_seq,)), dma((n_seq,)),
            dma((n_voc,)), dma((n_voc,)), dma((n_seq,)), dma((n_seq,)),
            dma((halves,)), dma((halves,)),
            dma((halves, n_seq)), dma((group,)),
            dma((n_voc,)), dma((n_voc,)),
        ],
        compiler_params=pltpu.CompilerParams(
            collective_id=0, has_side_effects=True, vmem_limit_bytes=54 * 1024 * 1024
        ),
        cost_estimate=pl.CostEstimate(
            flops=4 * slots * depth * vocab, bytes_accessed=2 * depth * vocab, transcendentals=2 * slots * vocab
        ),
        name="front",
    )(positions, counts, hidden, teacher, head_weight.T)

    rows = 256
    head = pl.pallas_call(
        head_kernel,
        out_shape=jax.ShapeDtypeStruct((vocab, depth), BF16),
        grid=(pl.cdiv(vocab, rows),),
        in_specs=[
            pl.BlockSpec((slots, rows), lambda i: (0, i)),
            pl.BlockSpec((slots, depth), lambda i: (0, 0)),
        ],
        out_specs=pl.BlockSpec((rows, depth), lambda i: (i, 0)),
        compiler_params=pltpu.CompilerParams(vmem_limit_bytes=40 * 1024 * 1024),
        cost_estimate=pl.CostEstimate(
            flops=2 * slots * depth * vocab, bytes_accessed=2 * depth * vocab, transcendentals=0
        ),
        name="head",
    )(grad, picked)
    return gh.astype(BF16), head.T


def solution(mesh):
    return jax.shard_map(
        functools.partial(per_device, mesh.shape["seq"], mesh.shape["vocab"]),
        mesh=mesh,
        in_specs=(
            P("seq", None),
            P(None, ("seq", "vocab")),
            P(None, ("seq", "vocab")),
            P("seq", None),
            P("seq"),
        ),
        out_specs=(P(("seq", "vocab"), None), P(None, ("seq", "vocab"))),
        check_vma=False,
    )
```

```python
import functools

import jax
import jax.numpy as jnp
from jax import lax
from jax.experimental import pallas as pl
from jax.experimental.pallas import tpu as pltpu
from jax.sharding import PartitionSpec as P

MESH = pl.DeviceIdType.MESH
LOSS_SCALE = 1024.0
F32 = jnp.float32
BF16 = jnp.bfloat16


def chunks_of(size, step):
    if size % 16:
        return 0, 0, size
    full = size // step
    return full, full * step, size - full * step


def front_kernel(
    n_seq, n_voc, step,
    pos_ref, cnt_ref, hid_ref, tea_ref, w_hbm,
    picked_ref, grad_ref, gh_ref,
    w_ref, gb, picked, stu, tex, grad, st1, st2, xs, xr, bs, br, cg, gh32,
    w_sem, g1s, g1r, g2s, g2r, s1s, s1r, s2s, s2r, as_, ar, bss, bsr, cs, cr, out_sem,
):
    slots, vocab = tea_ref.shape
    depth = hid_ref.shape[1]
    cap = pos_ref.shape[1]
    half = depth // 2
    quart = depth // 4
    own_cols = depth // n_voc
    sub = own_cols // 2
    halves = n_voc // 2
    group = n_seq * halves
    lanes = st1.shape[2]
    s = lax.axis_index("seq")
    v = lax.axis_index("vocab")
    core = v % 2
    other = 1 - core
    pair = v + 1 - 2 * core
    hv = v // 2
    flat = s * halves + hv
    full, tail_at, tail = chunks_of(vocab, step)

    def w_copy(i):
        rows = pl.ds(pl.multiple_of(i * step, step), step)
        return pltpu.make_async_copy(w_hbm.at[rows], w_ref.at[rows], w_sem.at[i])

    def w_tail():
        if full == 0:
            return pltpu.make_async_copy(w_hbm, w_ref, w_sem.at[0])
        rows = pl.ds(tail_at, tail)
        return pltpu.make_async_copy(w_hbm.at[rows], w_ref.at[rows], w_sem.at[full])

    if full:
        @pl.loop(0, full)
        def _(i):
            w_copy(i).start()
    if tail:
        w_tail().start()

    barrier = pltpu.get_barrier_semaphore()

    @pl.loop(1, group)
    def _(k):
        to = (flat + k) % group
        pl.semaphore_signal(
            barrier, inc=1, device_id=(to // halves, 2 * (to % halves) + core), device_id_type=MESH
        )

    @pl.loop(0, halves)
    def _(k):
        pl.semaphore_signal(barrier, inc=1, device_id=(s, 2 * k + other), device_id_type=MESH)

    tokens = hid_ref.shape[0]
    at_row = lax.broadcasted_iota(jnp.int32, (cap, tokens), 0)
    at_tok = lax.broadcasted_iota(jnp.int32, (cap, tokens), 1)
    hot = jnp.zeros((cap, tokens), F32)
    for k in range(cap):
        hot = jnp.where((at_row == k) & (at_tok == pos_ref[0, k]), 1.0, hot)
    mine = jnp.dot(hot.astype(BF16), hid_ref[...], preferred_element_type=F32)
    for h in range(2):
        lo = mine[:, h * half : h * half + quart]
        hi = mine[:, h * half + quart : (h + 1) * half]
        gb[s, h] = jnp.concatenate([lo, hi], axis=0).astype(BF16)

    pl.semaphore_wait(barrier, group - 1 + halves)

    def gather1(k, frm):
        return pltpu.make_async_remote_copy(
            src_ref=gb.at[frm, core], dst_ref=gb.at[frm, core],
            send_sem=g1s.at[k], recv_sem=g1r.at[frm],
            device_id=((s + k) % n_seq, v), device_id_type=MESH,
        )

    def gather2(frm, col):
        return pltpu.make_async_remote_copy(
            src_ref=gb.at[frm, col], dst_ref=gb.at[frm, col],
            send_sem=g2s.at[frm], recv_sem=g2r.at[frm],
            device_id=(s, pair), device_id_type=MESH,
        )

    @pl.loop(1, n_seq)
    def _(k):
        gather1(k, s).start()

    def over(body, init):
        carry = init
        if full:
            carry = lax.fori_loop(
                0, full, lambda i, c: body(pl.ds(pl.multiple_of(i * step, step), step), c), carry
            )
        if tail:
            carry = body(pl.ds(tail_at, tail), carry)
        return carry

    low = jnp.full((slots, 1), -jnp.inf, F32)
    none = jnp.zeros((slots, 1), F32)
    top_t = over(
        lambda at, c: jnp.maximum(c, jnp.max(tea_ref[:, at].astype(F32), axis=1, keepdims=True)), low
    )

    def teacher_total(at, c):
        e = jnp.exp(tea_ref[:, at].astype(F32) - top_t)
        tex[:, at] = e
        return c + jnp.sum(e, axis=1, keepdims=True)

    tot_t = over(teacher_total, none)

    @pl.loop(1, n_seq)
    def _(k):
        frm = (s + n_seq - k) % n_seq
        gather1(k, frm).wait_recv()
        gather2(frm, core).start()

    @pl.loop(1, n_seq)
    def _(k):
        gather2((s + n_seq - k) % n_seq, other).wait_recv()

    @pl.loop(0, n_seq // 2)
    def _(i):
        rows = pl.ds(pl.multiple_of(i * 2 * cap, 2 * cap), 2 * cap)
        for h in range(2):
            a = gb[2 * i, h].astype(F32)
            b = gb[2 * i + 1, h].astype(F32)
            for j in range(2):
                both = jnp.concatenate([a[j * cap : (j + 1) * cap], b[j * cap : (j + 1) * cap]], axis=0)
                picked[rows, h * half + j * quart : h * half + (j + 1) * quart] = both.astype(BF16)

    picked_out = pltpu.make_async_copy(picked, picked_ref, out_sem.at[0])
    picked_out.start()

    def student(at, top):
        block = lax.dot_general(
            w_ref[at, :], picked[...], (((1,), (1,)), ((), ())), preferred_element_type=F32
        )
        block = block.T
        stu[:, at] = block
        return jnp.maximum(top, jnp.max(block, axis=1, keepdims=True))

    top_s = low
    if full:
        def student_step(i, top):
            w_copy(i).wait()
            return student(pl.ds(pl.multiple_of(i * step, step), step), top)

        top_s = lax.fori_loop(0, full, student_step, top_s)
    if tail:
        w_tail().wait()
        top_s = student(pl.ds(tail_at, tail), top_s)

    def student_total(at, c):
        e = jnp.exp(stu[:, at] - top_s)
        stu[:, at] = e
        return c + jnp.sum(e, axis=1, keepdims=True)

    tot_s = over(student_total, none)

    lane = lax.broadcasted_iota(jnp.int32, (slots, 128), 1)
    wide = jnp.where(lane == 0, top_s, jnp.where(lane == 1, tot_s, jnp.where(lane == 2, top_t, tot_t)))
    if lanes > slots:
        wide = jnp.concatenate([wide, jnp.zeros((lanes - slots, 128), F32)], axis=0)
    st1[v] = wide.T[0:8, :]

    def stats1(k, frm):
        return pltpu.make_async_remote_copy(
            src_ref=st1.at[frm], dst_ref=st1.at[frm],
            send_sem=s1s.at[k], recv_sem=s1r.at[frm],
            device_id=(s, (v + k) % n_voc), device_id_type=MESH,
        )

    def stats2(k, frm):
        return pltpu.make_async_remote_copy(
            src_ref=st2.at[frm], dst_ref=st2.at[frm],
            send_sem=s2s.at[k], recv_sem=s2r.at[frm],
            device_id=((s + k) % n_seq, v), device_id_type=MESH,
        )

    def merge(ref):
        x = ref[...]
        ms, zs, mt, zt = x[:, 0:1, :], x[:, 1:2, :], x[:, 2:3, :], x[:, 3:4, :]
        top1 = jnp.max(ms, axis=0)
        top2 = jnp.max(mt, axis=0)
        return (
            top1, jnp.sum(zs * jnp.exp(ms - top1[None]), axis=0),
            top2, jnp.sum(zt * jnp.exp(mt - top2[None]), axis=0),
            jnp.sum(x[:, 4:5, :], axis=0),
        )

    for k in range(1, n_voc):
        stats1(k, v).start()
    for k in range(1, n_voc):
        stats1(k, (v + n_voc - k) % n_voc).wait_recv()
    slot_lane = lax.broadcasted_iota(jnp.int32, (1, lanes), 1)
    count = cnt_ref[0].astype(F32)
    my_count = jnp.where(slot_lane // cap == s, count, 0.0)
    m1, z1, m2, z2, _ = merge(st1)
    st2[s] = jnp.concatenate([m1, z1, m2, z2, my_count, jnp.zeros((3, lanes), F32)], axis=0)

    @pl.loop(1, n_seq)
    def _(k):
        stats2(k, s).start()

    @pl.loop(1, n_seq)
    def _(k):
        stats2(k, (s + n_seq - k) % n_seq).wait_recv()

    m1, z1, m2, z2, counts = merge(st2)
    weight = jnp.where(
        (slot_lane % cap).astype(F32) < counts, LOSS_SCALE / jnp.maximum(counts, 1.0), 0.0
    )
    rows = jnp.concatenate([m1, weight / z1, m2, weight / z2, jnp.zeros((124, lanes), F32)], axis=0)
    cols = rows.T[0:slots]
    scale_s = cols[:, 1:2] * jnp.exp(top_s - cols[:, 0:1])
    scale_t = cols[:, 3:4] * jnp.exp(top_t - cols[:, 2:3])

    def logits(at, c):
        grad[:, at] = (scale_s * stu[:, at] - scale_t * tex[:, at]).astype(BF16)
        return c

    over(logits, 0)
    grad_out = pltpu.make_async_copy(grad, grad_ref, out_sem.at[1])
    grad_out.start()

    def part(q, store):
        @pl.loop(0, 2)
        def _(j):
            at = pl.ds(pl.multiple_of(q * own_cols + j * sub, sub), sub)
            store(j, jnp.dot(grad[...], w_ref[:, at], preferred_element_type=F32))

    def to_pair(i):
        return pltpu.make_async_remote_copy(
            src_ref=xs.at[i], dst_ref=xr.at[i], send_sem=as_.at[i], recv_sem=ar.at[i],
            device_id=(s, pair), device_id_type=MESH,
        )

    def to_owner(i, k):
        h = (hv + 1 + i) % halves
        seq = (s + k) % n_seq
        return pltpu.make_async_remote_copy(
            src_ref=bs.at[i, seq], dst_ref=br.at[flat],
            send_sem=bss.at[i, k], recv_sem=bsr.at[flat],
            device_id=(seq, 2 * h + core), device_id_type=MESH,
        )

    for i in range(halves):
        h = (hv + 1 + i) % halves

        def store_pair(j, value, i=i):
            xs[i, j] = value

        part(2 * h + other, store_pair)
        to_pair(i).start()

        def store_own(j, value, i=i):
            for q in range(n_seq):
                bs32 = value[q * cap : (q + 1) * cap]
                gh32[q, pl.ds(pl.multiple_of(j * cap, cap), cap), :] = bs32

        part(2 * h + core, store_own)
        to_pair(i).wait_recv()
        for q in range(n_seq):
            for_q = [xr[i, j, q * cap : (q + 1) * cap, :] for j in range(2)]
            bs[i, q] = (gh32[q] + jnp.concatenate(for_q, axis=0)).astype(BF16)
        last = i == halves - 1
        for k in range(1 if last else 0, n_seq):
            to_owner(i, k).start()

    br[flat] = bs[halves - 1, s]

    def got(k):
        frm = (flat + k) % group
        return pltpu.make_async_remote_copy(
            src_ref=bs.at[0, 0], dst_ref=br.at[frm],
            send_sem=bss.at[0, 0], recv_sem=bsr.at[frm],
            device_id=(frm // halves, 2 * (frm % halves) + core), device_id_type=MESH,
        )

    @pl.loop(1, group)
    def _(k):
        got(k).wait_recv()

    total = lax.fori_loop(
        0, group, lambda k, c: c + br[k].astype(F32), jnp.zeros((2 * cap, sub), F32)
    )
    cg[v] = total.astype(BF16)

    def to_row(k, frm):
        return pltpu.make_async_remote_copy(
            src_ref=cg.at[frm], dst_ref=cg.at[frm], send_sem=cs.at[k], recv_sem=cr.at[frm],
            device_id=(s, (v + k) % n_voc), device_id_type=MESH,
        )

    for k in range(1, n_voc):
        to_row(k, v).start()
    for k in range(1, n_voc):
        to_row(k, (v + n_voc - k) % n_voc).wait_recv()
    per = cap // n_voc
    row_at = lax.broadcasted_iota(jnp.int32, (cap, sub), 0)
    for r in range(per):
        for q in range(n_voc):
            both = cg[q].astype(F32)
            for j in range(2):
                row = jnp.sum(
                    jnp.where(row_at == per * v + r, both[j * cap : (j + 1) * cap], 0.0),
                    axis=0, keepdims=True,
                )
                gh_ref[r : r + 1, q * own_cols + j * sub : q * own_cols + (j + 1) * sub] = row

    picked_out.wait()
    grad_out.wait()
    @pl.loop(1, n_seq)
    def _(k):
        gather1(k, s).wait_send()
        gather2((s + n_seq - k) % n_seq, core).wait_send()
        stats2(k, s).wait_send()

    for k in range(1, n_voc):
        stats1(k, v).wait_send()
        to_row(k, v).wait_send()
    for i in range(halves):
        to_pair(i).wait_send()
        for k in range(1 if i == halves - 1 else 0, n_seq):
            to_owner(i, k).wait_send()


def head_kernel(
    step, g_hbm, p_hbm, gh32_hbm, out_hbm, gh_ref, g_ref, p_ref, gh32_ref, buf, sem, in_sem
):
    taken = [
        pltpu.make_async_copy(src, dst, in_sem.at[i])
        for i, (src, dst) in enumerate(((g_hbm, g_ref), (p_hbm, p_ref), (gh32_hbm, gh32_ref)))
    ]
    for one in taken:
        one.start()
    for one in taken:
        one.wait()
    gh_ref[...] = gh32_ref[...].astype(BF16)
    vocab = g_ref.shape[1]
    full, tail_at, tail = chunks_of(vocab, step)

    def fill(at):
        buf[at, :] = lax.dot_general(
            g_ref[:, at], p_ref[...], (((0,), (0,)), ((), ())), preferred_element_type=F32
        ).astype(BF16)

    def copy(i):
        rows = pl.ds(pl.multiple_of(i * step, step), step)
        return pltpu.make_async_copy(buf.at[rows], out_hbm.at[rows], sem.at[i])

    def copy_tail():
        if full == 0:
            return pltpu.make_async_copy(buf, out_hbm, sem.at[0])
        rows = pl.ds(tail_at, tail)
        return pltpu.make_async_copy(buf.at[rows], out_hbm.at[rows], sem.at[full])

    if full:
        @pl.loop(0, full)
        def _(i):
            fill(pl.ds(pl.multiple_of(i * step, step), step))
            copy(i).start()
    if tail:
        fill(pl.ds(tail_at, tail))
        copy_tail().start()
    if full:
        @pl.loop(0, full)
        def _(i):
            copy(i).wait()
    if tail:
        copy_tail().wait()


def per_device(n_seq, n_voc, hidden, head_weight, teacher, positions, counts):
    slots, vocab = teacher.shape
    depth = hidden.shape[1]
    cap = positions.shape[1]
    halves = n_voc // 2
    group = n_seq * halves
    sub = depth // n_voc // 2
    lanes = -(-slots // 128) * 128
    step = 1024
    n_chunks = chunks_of(vocab, step)[0] + 1
    vmem = pl.BlockSpec(memory_space=pltpu.VMEM)
    smem = pl.BlockSpec(memory_space=pltpu.SMEM)
    anywhere = pl.BlockSpec(memory_space=pl.ANY)
    dma = pltpu.SemaphoreType.DMA
    picked, grad, gh = pl.pallas_call(
        functools.partial(front_kernel, n_seq, n_voc, step),
        out_shape=(
            jax.ShapeDtypeStruct((slots, depth), BF16),
            jax.ShapeDtypeStruct((slots, vocab), BF16),
            jax.ShapeDtypeStruct((cap // n_voc, depth), F32),
        ),
        in_specs=[smem, smem, vmem, vmem, pl.BlockSpec(memory_space=pl.ANY)],
        out_specs=(anywhere, anywhere, vmem),
        scratch_shapes=[
            pltpu.VMEM((vocab, depth), BF16),
            pltpu.VMEM((n_seq, 2, 2 * cap, depth // 4), BF16),
            pltpu.VMEM((slots, depth), BF16),
            pltpu.VMEM((slots, vocab), F32),
            pltpu.VMEM((slots, vocab), F32),
            pltpu.VMEM((slots, vocab), BF16),
            pltpu.VMEM((n_voc, 8, lanes), F32),
            pltpu.VMEM((n_seq, 8, lanes), F32),
            pltpu.VMEM((halves, 2, slots, sub), F32),
            pltpu.VMEM((halves, 2, slots, sub), F32),
            pltpu.VMEM((halves, n_seq, 2 * cap, sub), BF16),
            pltpu.VMEM((group, 2 * cap, sub), BF16),
            pltpu.VMEM((n_voc, 2 * cap, sub), BF16),
            pltpu.VMEM((n_seq, 2 * cap, sub), F32),
            dma((n_chunks,)),
            dma((n_seq,)), dma((n_seq,)), dma((n_seq,)), dma((n_seq,)),
            dma((n_voc,)), dma((n_voc,)), dma((n_seq,)), dma((n_seq,)),
            dma((halves,)), dma((halves,)),
            dma((halves, n_seq)), dma((group,)),
            dma((n_voc,)), dma((n_voc,)), dma((2,)),
        ],
        compiler_params=pltpu.CompilerParams(
            collective_id=0, has_side_effects=True, vmem_limit_bytes=54 * 1024 * 1024
        ),
        cost_estimate=pl.CostEstimate(
            flops=4 * slots * depth * vocab, bytes_accessed=2 * depth * vocab, transcendentals=2 * slots * vocab
        ),
        name="front",
    )(positions, counts, hidden, teacher, head_weight.T)

    rows = 512
    head, gh = pl.pallas_call(
        functools.partial(head_kernel, rows),
        out_shape=(
            jax.ShapeDtypeStruct((vocab, depth), BF16),
            jax.ShapeDtypeStruct((cap // n_voc, depth), BF16),
        ),
        in_specs=[anywhere, anywhere, anywhere],
        out_specs=(anywhere, vmem),
        scratch_shapes=[
            pltpu.VMEM((slots, vocab), BF16),
            pltpu.VMEM((slots, depth), BF16),
            pltpu.VMEM((cap // n_voc, depth), F32),
            pltpu.VMEM((vocab, depth), BF16),
            dma((chunks_of(vocab, rows)[0] + 1,)),
            dma((3,)),
        ],
        compiler_params=pltpu.CompilerParams(vmem_limit_bytes=48 * 1024 * 1024),
        cost_estimate=pl.CostEstimate(
            flops=2 * slots * depth * vocab, bytes_accessed=2 * depth * vocab, transcendentals=0
        ),
        name="head",
    )(grad, picked, gh)
    return gh, head.T


def solution(mesh):
    return jax.shard_map(
        functools.partial(per_device, mesh.shape["seq"], mesh.shape["vocab"]),
        mesh=mesh,
        in_specs=(
            P("seq", None),
            P(None, ("seq", "vocab")),
            P(None, ("seq", "vocab")),
            P("seq", None),
            P("seq"),
        ),
        out_specs=(P(("seq", "vocab"), None), P(None, ("seq", "vocab"))),
        check_vma=False,
    )
```

```python
import functools

import jax
import jax.numpy as jnp
from jax import lax
from jax.experimental import pallas as pl
from jax.experimental.pallas import tpu as pltpu
from jax.sharding import PartitionSpec as P

MESH = pl.DeviceIdType.MESH
LOSS_SCALE = 1024.0
F32 = jnp.float32
BF16 = jnp.bfloat16


def chunks_of(size, step):
    if size % 16:
        return 0, 0, size
    full = size // step
    return full, full * step, size - full * step


def front_kernel(
    n_seq, n_voc, step,
    pos_ref, cnt_ref, hid_ref, tea_ref, w_hbm,
    picked_ref, grad_ref, gh_ref,
    w_ref, gb, picked, stu, tex, grad, exps, sums, st1, st2, xs, xr, bs, br, cg,
    w_sem, g1s, g1r, g2s, g2r, s1s, s1r, s2s, s2r, as_, ar, bss, bsr, cs, cr, out_sem,
):
    slots, vocab = tea_ref.shape
    depth = hid_ref.shape[1]
    cap = pos_ref.shape[1]
    half = depth // 2
    quart = depth // 4
    own_cols = depth // n_voc
    sub = own_cols // 2
    halves = n_voc // 2
    group = n_seq * halves
    lanes = st1.shape[2]
    s = lax.axis_index("seq")
    v = lax.axis_index("vocab")
    core = v % 2
    other = 1 - core
    pair = v + 1 - 2 * core
    hv = v // 2
    flat = s * halves + hv
    full, tail_at, tail = chunks_of(vocab, step)

    def w_copy(i):
        rows = pl.ds(pl.multiple_of(i * step, step), step)
        return pltpu.make_async_copy(w_hbm.at[rows], w_ref.at[rows], w_sem.at[i])

    def w_tail():
        if full == 0:
            return pltpu.make_async_copy(w_hbm, w_ref, w_sem.at[0])
        rows = pl.ds(tail_at, tail)
        return pltpu.make_async_copy(w_hbm.at[rows], w_ref.at[rows], w_sem.at[full])

    if full:
        @pl.loop(0, full)
        def _(i):
            w_copy(i).start()
    if tail:
        w_tail().start()

    barrier = pltpu.get_barrier_semaphore()

    @pl.loop(1, group)
    def _(k):
        to = (flat + k) % group
        pl.semaphore_signal(
            barrier, inc=1, device_id=(to // halves, 2 * (to % halves) + core), device_id_type=MESH
        )

    @pl.loop(0, halves)
    def _(k):
        pl.semaphore_signal(barrier, inc=1, device_id=(s, 2 * k + other), device_id_type=MESH)

    tokens = hid_ref.shape[0]
    at_row = lax.broadcasted_iota(jnp.int32, (cap, tokens), 0)
    at_tok = lax.broadcasted_iota(jnp.int32, (cap, tokens), 1)
    hot = jnp.zeros((cap, tokens), F32)
    for k in range(cap):
        hot = jnp.where((at_row == k) & (at_tok == pos_ref[0, k]), 1.0, hot)
    mine = jnp.dot(hot.astype(BF16), hid_ref[...], preferred_element_type=F32)
    for h in range(2):
        lo = mine[:, h * half : h * half + quart]
        hi = mine[:, h * half + quart : (h + 1) * half]
        gb[s, h] = jnp.concatenate([lo, hi], axis=0).astype(BF16)

    pl.semaphore_wait(barrier, group - 1 + halves)

    def gather1(k, frm):
        return pltpu.make_async_remote_copy(
            src_ref=gb.at[frm, core], dst_ref=gb.at[frm, core],
            send_sem=g1s.at[k], recv_sem=g1r.at[frm],
            device_id=((s + k) % n_seq, v), device_id_type=MESH,
        )

    def gather2(frm, col):
        return pltpu.make_async_remote_copy(
            src_ref=gb.at[frm, col], dst_ref=gb.at[frm, col],
            send_sem=g2s.at[frm], recv_sem=g2r.at[frm],
            device_id=(s, pair), device_id_type=MESH,
        )

    @pl.loop(1, n_seq)
    def _(k):
        gather1(k, s).start()

    def over(body, init):
        carry = init
        if full:
            carry = lax.fori_loop(
                0, full, lambda i, c: body(pl.ds(pl.multiple_of(i * step, step), step), c), carry
            )
        if tail:
            carry = body(pl.ds(tail_at, tail), carry)
        return carry

    low = jnp.full((slots, 1), -jnp.inf, F32)
    none = jnp.zeros((slots, 1), F32)
    top_t = over(
        lambda at, c: jnp.maximum(c, jnp.max(tea_ref[:, at].astype(F32), axis=1, keepdims=True)), low
    )

    def split(i, at, e):
        near = e.astype(BF16)
        exps[i * slots : (i + 1) * slots, at] = near
        exps[(i + 1) * slots : (i + 2) * slots, at] = (e - near.astype(F32)).astype(BF16)

    def teacher_total(at, c):
        e = jnp.exp(tea_ref[:, at].astype(F32) - top_t)
        tex[:, at] = e
        split(2, at, e)
        return c + jnp.sum(e, axis=1, keepdims=True)

    tot_t = over(teacher_total, none)

    @pl.loop(1, n_seq)
    def _(k):
        frm = (s + n_seq - k) % n_seq
        gather1(k, frm).wait_recv()
        gather2(frm, core).start()

    @pl.loop(1, n_seq)
    def _(k):
        gather2((s + n_seq - k) % n_seq, other).wait_recv()

    @pl.loop(0, n_seq // 2)
    def _(i):
        rows = pl.ds(pl.multiple_of(i * 2 * cap, 2 * cap), 2 * cap)
        for h in range(2):
            a = gb[2 * i, h].astype(F32)
            b = gb[2 * i + 1, h].astype(F32)
            for j in range(2):
                both = jnp.concatenate([a[j * cap : (j + 1) * cap], b[j * cap : (j + 1) * cap]], axis=0)
                picked[rows, h * half + j * quart : h * half + (j + 1) * quart] = both.astype(BF16)

    picked_out = pltpu.make_async_copy(picked, picked_ref, out_sem.at[0])
    picked_out.start()

    def student(at, top):
        block = lax.dot_general(
            w_ref[at, :], picked[...], (((1,), (1,)), ((), ())), preferred_element_type=F32
        )
        block = block.T
        stu[:, at] = block
        return jnp.maximum(top, jnp.max(block, axis=1, keepdims=True))

    top_s = low
    if full:
        def student_step(i, top):
            w_copy(i).wait()
            return student(pl.ds(pl.multiple_of(i * step, step), step), top)

        top_s = lax.fori_loop(0, full, student_step, top_s)
    if tail:
        w_tail().wait()
        top_s = student(pl.ds(tail_at, tail), top_s)

    def student_total(at, c):
        e = jnp.exp(stu[:, at] - top_s)
        stu[:, at] = e
        split(0, at, e)
        return c + jnp.sum(e, axis=1, keepdims=True)

    tot_s = over(student_total, none)

    lane = lax.broadcasted_iota(jnp.int32, (slots, 128), 1)
    wide = jnp.where(lane == 0, top_s, jnp.where(lane == 1, tot_s, jnp.where(lane == 2, top_t, tot_t)))
    if lanes > slots:
        wide = jnp.concatenate([wide, jnp.zeros((lanes - slots, 128), F32)], axis=0)
    st1[v] = wide.T[0:8, :]

    def stats1(k, frm):
        return pltpu.make_async_remote_copy(
            src_ref=st1.at[frm], dst_ref=st1.at[frm],
            send_sem=s1s.at[k], recv_sem=s1r.at[frm],
            device_id=(s, (v + k) % n_voc), device_id_type=MESH,
        )

    def stats2(k, frm):
        return pltpu.make_async_remote_copy(
            src_ref=st2.at[frm], dst_ref=st2.at[frm],
            send_sem=s2s.at[k], recv_sem=s2r.at[frm],
            device_id=((s + k) % n_seq, v), device_id_type=MESH,
        )

    def merge(ref):
        x = ref[...]
        ms, zs, mt, zt = x[:, 0:1, :], x[:, 1:2, :], x[:, 2:3, :], x[:, 3:4, :]
        top1 = jnp.max(ms, axis=0)
        top2 = jnp.max(mt, axis=0)
        return (
            top1, jnp.sum(zs * jnp.exp(ms - top1[None]), axis=0),
            top2, jnp.sum(zt * jnp.exp(mt - top2[None]), axis=0),
            jnp.sum(x[:, 4:5, :], axis=0),
        )

    def half_of(i):
        return (hv + 1 + i) % halves

    def part(i, mine):
        q = 2 * half_of(i) + (core if mine else other)

        @pl.loop(0, 2)
        def _(j):
            at = pl.ds(pl.multiple_of(q * own_cols + j * sub, sub), sub)
            out = jnp.dot(exps[...], w_ref[:, at], preferred_element_type=F32)
            sums[0, 2 * i + mine, j] = out[0:slots] + out[slots : 2 * slots]
            sums[1, 2 * i + mine, j] = out[2 * slots : 3 * slots] + out[3 * slots :]

    def to_pair(i):
        return pltpu.make_async_remote_copy(
            src_ref=xs.at[i], dst_ref=xr.at[i], send_sem=as_.at[i], recv_sem=ar.at[i],
            device_id=(s, pair), device_id_type=MESH,
        )

    def to_owner(i, k):
        seq = (s + k) % n_seq
        return pltpu.make_async_remote_copy(
            src_ref=bs.at[i, seq], dst_ref=br.at[flat],
            send_sem=bss.at[i, k], recv_sem=bsr.at[flat],
            device_id=(seq, 2 * half_of(i) + core), device_id_type=MESH,
        )

    for k in range(1, n_voc):
        stats1(k, v).start()
    part(0, 0)
    for k in range(1, n_voc):
        stats1(k, (v + n_voc - k) % n_voc).wait_recv()
    slot_lane = lax.broadcasted_iota(jnp.int32, (1, lanes), 1)
    count = cnt_ref[0].astype(F32)
    my_count = jnp.where(slot_lane // cap == s, count, 0.0)
    m1, z1, m2, z2, _ = merge(st1)
    st2[s] = jnp.concatenate([m1, z1, m2, z2, my_count, jnp.zeros((3, lanes), F32)], axis=0)

    @pl.loop(1, n_seq)
    def _(k):
        stats2(k, s).start()

    part(0, 1)

    @pl.loop(1, n_seq)
    def _(k):
        stats2(k, (s + n_seq - k) % n_seq).wait_recv()

    m1, z1, m2, z2, counts = merge(st2)
    weight = jnp.where(
        (slot_lane % cap).astype(F32) < counts, LOSS_SCALE / jnp.maximum(counts, 1.0), 0.0
    )
    rows = jnp.concatenate([m1, weight / z1, m2, weight / z2, jnp.zeros((124, lanes), F32)], axis=0)
    cols = rows.T[0:slots]
    scale_s = cols[:, 1:2] * jnp.exp(top_s - cols[:, 0:1])
    scale_t = cols[:, 3:4] * jnp.exp(top_t - cols[:, 2:3])

    def scaled(i, mine, j):
        return scale_s * sums[0, 2 * i + mine, j] - scale_t * sums[1, 2 * i + mine, j]

    def send_pair(i):
        for j in range(2):
            xs[i, j] = scaled(i, 0, j)
        to_pair(i).start()

    def send_owners(i):
        to_pair(i).wait_recv()
        both = [scaled(i, 1, j) + xr[i, j] for j in range(2)]
        for q in range(n_seq):
            rows_q = [x[q * cap : (q + 1) * cap] for x in both]
            bs[i, q] = jnp.concatenate(rows_q, axis=0).astype(BF16)
        for k in range(1 if i == halves - 1 else 0, n_seq):
            to_owner(i, k).start()

    def logits(at, c):
        grad[:, at] = (scale_s * stu[:, at] - scale_t * tex[:, at]).astype(BF16)
        return c

    send_pair(0)
    grad_out = pltpu.make_async_copy(grad, grad_ref, out_sem.at[1])
    over(logits, 0)
    grad_out.start()
    for i in range(1, halves):
        part(i, 0)
        send_pair(i)
        send_owners(i - 1)
        part(i, 1)
    send_owners(halves - 1)

    br[flat] = bs[halves - 1, s]

    def got(k):
        frm = (flat + k) % group
        return pltpu.make_async_remote_copy(
            src_ref=bs.at[0, 0], dst_ref=br.at[frm],
            send_sem=bss.at[0, 0], recv_sem=bsr.at[frm],
            device_id=(frm // halves, 2 * (frm % halves) + core), device_id_type=MESH,
        )

    @pl.loop(1, group)
    def _(k):
        got(k).wait_recv()

    total = lax.fori_loop(
        0, group, lambda k, c: c + br[k].astype(F32), jnp.zeros((2 * cap, sub), F32)
    )
    cg[v] = total.astype(BF16)

    def to_row(k, frm):
        return pltpu.make_async_remote_copy(
            src_ref=cg.at[frm], dst_ref=cg.at[frm], send_sem=cs.at[k], recv_sem=cr.at[frm],
            device_id=(s, (v + k) % n_voc), device_id_type=MESH,
        )

    for k in range(1, n_voc):
        to_row(k, v).start()
    for k in range(1, n_voc):
        to_row(k, (v + n_voc - k) % n_voc).wait_recv()
    per = cap // n_voc
    row_at = lax.broadcasted_iota(jnp.int32, (cap, sub), 0)
    for r in range(per):
        for q in range(n_voc):
            both = cg[q].astype(F32)
            for j in range(2):
                row = jnp.sum(
                    jnp.where(row_at == per * v + r, both[j * cap : (j + 1) * cap], 0.0),
                    axis=0, keepdims=True,
                )
                gh_ref[r : r + 1, q * own_cols + j * sub : q * own_cols + (j + 1) * sub] = row

    picked_out.wait()
    grad_out.wait()
    @pl.loop(1, n_seq)
    def _(k):
        gather1(k, s).wait_send()
        gather2((s + n_seq - k) % n_seq, core).wait_send()
        stats2(k, s).wait_send()

    for k in range(1, n_voc):
        stats1(k, v).wait_send()
        to_row(k, v).wait_send()
    for i in range(halves):
        to_pair(i).wait_send()
        for k in range(1 if i == halves - 1 else 0, n_seq):
            to_owner(i, k).wait_send()


def head_kernel(
    step, g_hbm, p_hbm, gh32_hbm, out_hbm, gh_ref, g_ref, gt_ref, p_ref, gh32_ref, buf, sem, in_sem
):
    taken = [
        pltpu.make_async_copy(src, dst, in_sem.at[i])
        for i, (src, dst) in enumerate(((g_hbm, g_ref), (p_hbm, p_ref), (gh32_hbm, gh32_ref)))
    ]
    for one in taken:
        one.start()
    for one in taken:
        one.wait()
    gh_ref[...] = gh32_ref[...].astype(BF16)
    vocab = g_ref.shape[1]
    full, tail_at, tail = chunks_of(vocab, step)

    def turn(at):
        gt_ref[at, :] = g_ref[:, at].T

    def fill(at):
        buf[at, :] = jnp.dot(gt_ref[at, :], p_ref[...], preferred_element_type=F32).astype(BF16)

    def rows_of(i):
        return pl.ds(pl.multiple_of(i * step, step), step)

    def copy(i):
        rows = pl.ds(pl.multiple_of(i * step, step), step)
        return pltpu.make_async_copy(buf.at[rows], out_hbm.at[rows], sem.at[i])

    def copy_tail():
        if full == 0:
            return pltpu.make_async_copy(buf, out_hbm, sem.at[0])
        rows = pl.ds(tail_at, tail)
        return pltpu.make_async_copy(buf.at[rows], out_hbm.at[rows], sem.at[full])

    if full:
        turn(rows_of(0))

        @pl.loop(0, full - 1)
        def _(i):
            turn(rows_of(i + 1))
            fill(rows_of(i))
            copy(i).start()

    if tail:
        turn(pl.ds(tail_at, tail))
    if full:
        fill(rows_of(full - 1))
        copy(full - 1).start()
    if tail:
        fill(pl.ds(tail_at, tail))
        copy_tail().start()
    if full:
        @pl.loop(0, full)
        def _(i):
            copy(i).wait()
    if tail:
        copy_tail().wait()


def per_device(n_seq, n_voc, hidden, head_weight, teacher, positions, counts):
    slots, vocab = teacher.shape
    depth = hidden.shape[1]
    cap = positions.shape[1]
    halves = n_voc // 2
    group = n_seq * halves
    sub = depth // n_voc // 2
    lanes = -(-slots // 128) * 128
    step = 1024
    n_chunks = chunks_of(vocab, step)[0] + 1
    vmem = pl.BlockSpec(memory_space=pltpu.VMEM)
    smem = pl.BlockSpec(memory_space=pltpu.SMEM)
    anywhere = pl.BlockSpec(memory_space=pl.ANY)
    dma = pltpu.SemaphoreType.DMA
    picked, grad, gh = pl.pallas_call(
        functools.partial(front_kernel, n_seq, n_voc, step),
        out_shape=(
            jax.ShapeDtypeStruct((slots, depth), BF16),
            jax.ShapeDtypeStruct((slots, vocab), BF16),
            jax.ShapeDtypeStruct((cap // n_voc, depth), F32),
        ),
        in_specs=[smem, smem, vmem, vmem, pl.BlockSpec(memory_space=pl.ANY)],
        out_specs=(anywhere, anywhere, vmem),
        scratch_shapes=[
            pltpu.VMEM((vocab, depth), BF16),
            pltpu.VMEM((n_seq, 2, 2 * cap, depth // 4), BF16),
            pltpu.VMEM((slots, depth), BF16),
            pltpu.VMEM((slots, vocab), F32),
            pltpu.VMEM((slots, vocab), F32),
            pltpu.VMEM((slots, vocab), BF16),
            pltpu.VMEM((4 * slots, vocab), BF16),
            pltpu.VMEM((2, n_voc, 2, slots, sub), F32),
            pltpu.VMEM((n_voc, 8, lanes), F32),
            pltpu.VMEM((n_seq, 8, lanes), F32),
            pltpu.VMEM((halves, 2, slots, sub), F32),
            pltpu.VMEM((halves, 2, slots, sub), F32),
            pltpu.VMEM((halves, n_seq, 2 * cap, sub), BF16),
            pltpu.VMEM((group, 2 * cap, sub), BF16),
            pltpu.VMEM((n_voc, 2 * cap, sub), BF16),
            dma((n_chunks,)),
            dma((n_seq,)), dma((n_seq,)), dma((n_seq,)), dma((n_seq,)),
            dma((n_voc,)), dma((n_voc,)), dma((n_seq,)), dma((n_seq,)),
            dma((halves,)), dma((halves,)),
            dma((halves, n_seq)), dma((group,)),
            dma((n_voc,)), dma((n_voc,)), dma((2,)),
        ],
        compiler_params=pltpu.CompilerParams(
            collective_id=0, has_side_effects=True, vmem_limit_bytes=54 * 1024 * 1024
        ),
        cost_estimate=pl.CostEstimate(
            flops=4 * slots * depth * vocab, bytes_accessed=2 * depth * vocab, transcendentals=2 * slots * vocab
        ),
        name="front",
    )(positions, counts, hidden, teacher, head_weight.T)

    rows = 512
    head, gh = pl.pallas_call(
        functools.partial(head_kernel, rows),
        out_shape=(
            jax.ShapeDtypeStruct((vocab, depth), BF16),
            jax.ShapeDtypeStruct((cap // n_voc, depth), BF16),
        ),
        in_specs=[pl.BlockSpec(memory_space=pltpu.HBM)] * 3,
        out_specs=(anywhere, vmem),
        scratch_shapes=[
            pltpu.VMEM((slots, vocab), BF16),
            pltpu.VMEM((vocab, slots), BF16),
            pltpu.VMEM((slots, depth), BF16),
            pltpu.VMEM((cap // n_voc, depth), F32),
            pltpu.VMEM((vocab, depth), BF16),
            dma((chunks_of(vocab, rows)[0] + 1,)),
            dma((3,)),
        ],
        compiler_params=pltpu.CompilerParams(vmem_limit_bytes=60 * 1024 * 1024),
        cost_estimate=pl.CostEstimate(
            flops=2 * slots * depth * vocab, bytes_accessed=2 * depth * vocab, transcendentals=0
        ),
        name="head",
    )(grad, picked, gh)
    return gh, head.T


def solution(mesh):
    return jax.shard_map(
        functools.partial(per_device, mesh.shape["seq"], mesh.shape["vocab"]),
        mesh=mesh,
        in_specs=(
            P("seq", None),
            P(None, ("seq", "vocab")),
            P(None, ("seq", "vocab")),
            P("seq", None),
            P("seq"),
        ),
        out_specs=(P(("seq", "vocab"), None), P(None, ("seq", "vocab"))),
        check_vma=False,
    )
```

```python
import functools

import jax
import jax.numpy as jnp
from jax import lax
from jax.experimental import pallas as pl
from jax.experimental.pallas import tpu as pltpu
from jax.sharding import PartitionSpec as P

MESH = pl.DeviceIdType.MESH
LOSS_SCALE = 1024.0
F32 = jnp.float32
BF16 = jnp.bfloat16


def chunks_of(size, step):
    if size % 16:
        return 0, 0, size
    full = size // step
    return full, full * step, size - full * step


def front_kernel(
    n_seq, n_voc, step,
    pos_ref, cnt_ref, hid_ref, tea_ref, w_hbm,
    picked_ref, grad_ref, gh_ref,
    w_ref, gb, picked, stu, tex, grad, exps, sums, st1, st2, xs, xr, bs, br, cg,
    w_sem, g1s, g1r, g2s, g2r, s1s, s1r, s2s, s2r, as_, ar, bss, bsr, cs, cr, out_sem,
):
    slots, vocab = tea_ref.shape
    depth = hid_ref.shape[1]
    cap = pos_ref.shape[1]
    half = depth // 2
    quart = depth // 4
    own_cols = depth // n_voc
    sub = own_cols // 2
    halves = n_voc // 2
    group = n_seq * halves
    lanes = st1.shape[2]
    s = lax.axis_index("seq")
    v = lax.axis_index("vocab")
    core = v % 2
    other = 1 - core
    pair = v + 1 - 2 * core
    hv = v // 2
    flat = s * halves + hv
    full, tail_at, tail = chunks_of(vocab, step)

    def w_copy(i):
        rows = pl.ds(pl.multiple_of(i * step, step), step)
        return pltpu.make_async_copy(w_hbm.at[rows], w_ref.at[rows], w_sem.at[i])

    def w_tail():
        if full == 0:
            return pltpu.make_async_copy(w_hbm, w_ref, w_sem.at[0])
        rows = pl.ds(tail_at, tail)
        return pltpu.make_async_copy(w_hbm.at[rows], w_ref.at[rows], w_sem.at[full])

    if full:
        @pl.loop(0, full)
        def _(i):
            w_copy(i).start()
    if tail:
        w_tail().start()

    barrier = pltpu.get_barrier_semaphore()

    @pl.loop(1, group)
    def _(k):
        to = (flat + k) % group
        pl.semaphore_signal(
            barrier, inc=1, device_id=(to // halves, 2 * (to % halves) + core), device_id_type=MESH
        )

    @pl.loop(0, halves)
    def _(k):
        pl.semaphore_signal(barrier, inc=1, device_id=(s, 2 * k + other), device_id_type=MESH)

    tokens = hid_ref.shape[0]
    at_row = lax.broadcasted_iota(jnp.int32, (cap, tokens), 0)
    at_tok = lax.broadcasted_iota(jnp.int32, (cap, tokens), 1)
    hot = jnp.zeros((cap, tokens), F32)
    for k in range(cap):
        hot = jnp.where((at_row == k) & (at_tok == pos_ref[0, k]), 1.0, hot)
    mine = jnp.dot(hot.astype(BF16), hid_ref[...], preferred_element_type=F32)
    for h in range(2):
        lo = mine[:, h * half : h * half + quart]
        hi = mine[:, h * half + quart : (h + 1) * half]
        gb[s, h] = jnp.concatenate([lo, hi], axis=0).astype(BF16)

    pl.semaphore_wait(barrier, group - 1 + halves)

    def gather1(k, frm):
        return pltpu.make_async_remote_copy(
            src_ref=gb.at[frm, core], dst_ref=gb.at[frm, core],
            send_sem=g1s.at[k], recv_sem=g1r.at[frm],
            device_id=((s + k) % n_seq, v), device_id_type=MESH,
        )

    def gather2(frm, col):
        return pltpu.make_async_remote_copy(
            src_ref=gb.at[frm, col], dst_ref=gb.at[frm, col],
            send_sem=g2s.at[frm], recv_sem=g2r.at[frm],
            device_id=(s, pair), device_id_type=MESH,
        )

    @pl.loop(1, n_seq)
    def _(k):
        gather1(k, s).start()

    def over(body, init):
        carry = init
        if full:
            carry = lax.fori_loop(
                0, full, lambda i, c: body(pl.ds(pl.multiple_of(i * step, step), step), c), carry
            )
        if tail:
            carry = body(pl.ds(tail_at, tail), carry)
        return carry

    low = jnp.full((slots, 1), -jnp.inf, F32)
    none = jnp.zeros((slots, 1), F32)
    top_t = over(
        lambda at, c: jnp.maximum(c, jnp.max(tea_ref[:, at].astype(F32), axis=1, keepdims=True)), low
    )

    def split(i, at, e):
        near = e.astype(BF16)
        exps[i * slots : (i + 1) * slots, at] = near
        exps[(i + 1) * slots : (i + 2) * slots, at] = (e - near.astype(F32)).astype(BF16)

    def teacher_total(at, c):
        e = jnp.exp(tea_ref[:, at].astype(F32) - top_t)
        tex[:, at] = e
        split(2, at, e)
        return c + jnp.sum(e, axis=1, keepdims=True)

    tot_t = over(teacher_total, none)

    @pl.loop(1, n_seq)
    def _(k):
        frm = (s + n_seq - k) % n_seq
        gather1(k, frm).wait_recv()
        gather2(frm, core).start()

    @pl.loop(1, n_seq)
    def _(k):
        gather2((s + n_seq - k) % n_seq, other).wait_recv()

    @pl.loop(0, n_seq // 2)
    def _(i):
        rows = pl.ds(pl.multiple_of(i * 2 * cap, 2 * cap), 2 * cap)
        for h in range(2):
            a = gb[2 * i, h].astype(F32)
            b = gb[2 * i + 1, h].astype(F32)
            for j in range(2):
                both = jnp.concatenate([a[j * cap : (j + 1) * cap], b[j * cap : (j + 1) * cap]], axis=0)
                picked[rows, h * half + j * quart : h * half + (j + 1) * quart] = both.astype(BF16)

    picked_out = pltpu.make_async_copy(picked, picked_ref, out_sem.at[0])
    picked_out.start()

    def student(at, top):
        block = lax.dot_general(
            w_ref[at, :], picked[...], (((1,), (1,)), ((), ())), preferred_element_type=F32
        )
        block = block.T
        stu[:, at] = block
        return jnp.maximum(top, jnp.max(block, axis=1, keepdims=True))

    top_s = low
    if full:
        def student_step(i, top):
            w_copy(i).wait()
            return student(pl.ds(pl.multiple_of(i * step, step), step), top)

        top_s = lax.fori_loop(0, full, student_step, top_s)
    if tail:
        w_tail().wait()
        top_s = student(pl.ds(tail_at, tail), top_s)

    def student_total(at, c):
        e = jnp.exp(stu[:, at] - top_s)
        stu[:, at] = e
        split(0, at, e)
        return c + jnp.sum(e, axis=1, keepdims=True)

    tot_s = over(student_total, none)

    lane = lax.broadcasted_iota(jnp.int32, (slots, 128), 1)
    wide = jnp.where(lane == 0, top_s, jnp.where(lane == 1, tot_s, jnp.where(lane == 2, top_t, tot_t)))
    if lanes > slots:
        wide = jnp.concatenate([wide, jnp.zeros((lanes - slots, 128), F32)], axis=0)
    st1[v] = wide.T[0:8, :]

    def stats1(k, frm):
        return pltpu.make_async_remote_copy(
            src_ref=st1.at[frm], dst_ref=st1.at[frm],
            send_sem=s1s.at[k], recv_sem=s1r.at[frm],
            device_id=(s, (v + k) % n_voc), device_id_type=MESH,
        )

    def stats2(k, frm):
        return pltpu.make_async_remote_copy(
            src_ref=st2.at[frm], dst_ref=st2.at[frm],
            send_sem=s2s.at[k], recv_sem=s2r.at[frm],
            device_id=((s + k) % n_seq, v), device_id_type=MESH,
        )

    def merge(ref):
        x = ref[...]
        ms, zs, mt, zt = x[:, 0:1, :], x[:, 1:2, :], x[:, 2:3, :], x[:, 3:4, :]
        top1 = jnp.max(ms, axis=0)
        top2 = jnp.max(mt, axis=0)
        return (
            top1, jnp.sum(zs * jnp.exp(ms - top1[None]), axis=0),
            top2, jnp.sum(zt * jnp.exp(mt - top2[None]), axis=0),
            jnp.sum(x[:, 4:5, :], axis=0),
        )

    def half_of(i):
        return (hv + 1 + i) % halves

    def part(i, mine):
        q = 2 * half_of(i) + (core if mine else other)

        @pl.loop(0, 2)
        def _(j):
            at = pl.ds(pl.multiple_of(q * own_cols + j * sub, sub), sub)
            out = jnp.dot(exps[...], w_ref[:, at], preferred_element_type=F32)
            sums[0, 2 * i + mine, j] = out[0:slots] + out[slots : 2 * slots]
            sums[1, 2 * i + mine, j] = out[2 * slots : 3 * slots] + out[3 * slots :]

    def to_pair(i):
        return pltpu.make_async_remote_copy(
            src_ref=xs.at[i], dst_ref=xr.at[i], send_sem=as_.at[i], recv_sem=ar.at[i],
            device_id=(s, pair), device_id_type=MESH,
        )

    def to_owner(i, k):
        seq = (s + k) % n_seq
        return pltpu.make_async_remote_copy(
            src_ref=bs.at[i, seq], dst_ref=br.at[flat],
            send_sem=bss.at[i, k], recv_sem=bsr.at[flat],
            device_id=(seq, 2 * half_of(i) + core), device_id_type=MESH,
        )

    for k in range(1, n_voc):
        stats1(k, v).start()
    part(0, 0)
    for k in range(1, n_voc):
        stats1(k, (v + n_voc - k) % n_voc).wait_recv()
    slot_lane = lax.broadcasted_iota(jnp.int32, (1, lanes), 1)
    count = cnt_ref[0].astype(F32)
    my_count = jnp.where(slot_lane // cap == s, count, 0.0)
    m1, z1, m2, z2, _ = merge(st1)
    st2[s] = jnp.concatenate([m1, z1, m2, z2, my_count, jnp.zeros((3, lanes), F32)], axis=0)

    @pl.loop(1, n_seq)
    def _(k):
        stats2(k, s).start()

    part(0, 1)

    @pl.loop(1, n_seq)
    def _(k):
        stats2(k, (s + n_seq - k) % n_seq).wait_recv()

    m1, z1, m2, z2, counts = merge(st2)
    weight = jnp.where(
        (slot_lane % cap).astype(F32) < counts, LOSS_SCALE / jnp.maximum(counts, 1.0), 0.0
    )
    rows = jnp.concatenate([m1, weight / z1, m2, weight / z2, jnp.zeros((124, lanes), F32)], axis=0)
    cols = rows.T[0:slots]
    scale_s = cols[:, 1:2] * jnp.exp(top_s - cols[:, 0:1])
    scale_t = cols[:, 3:4] * jnp.exp(top_t - cols[:, 2:3])

    def scaled(i, mine, j):
        return scale_s * sums[0, 2 * i + mine, j] - scale_t * sums[1, 2 * i + mine, j]

    def send_pair(i):
        for j in range(2):
            xs[i, j] = scaled(i, 0, j)
        to_pair(i).start()

    def send_owners(i):
        to_pair(i).wait_recv()
        both = [scaled(i, 1, j) + xr[i, j] for j in range(2)]
        for q in range(n_seq):
            rows_q = [x[q * cap : (q + 1) * cap] for x in both]
            bs[i, q] = jnp.concatenate(rows_q, axis=0).astype(BF16)
        for k in range(1 if i == halves - 1 else 0, n_seq):
            to_owner(i, k).start()

    def logits(at, c):
        grad[:, at] = (scale_s * stu[:, at] - scale_t * tex[:, at]).astype(BF16)
        return c

    send_pair(0)
    for i in range(1, halves):
        part(i, 0)
        send_pair(i)
        send_owners(i - 1)
        part(i, 1)
    send_owners(halves - 1)

    over(logits, 0)
    grad_out = pltpu.make_async_copy(grad, grad_ref, out_sem.at[1])
    grad_out.start()

    br[flat] = bs[halves - 1, s]

    def got(k):
        frm = (flat + k) % group
        return pltpu.make_async_remote_copy(
            src_ref=bs.at[0, 0], dst_ref=br.at[frm],
            send_sem=bss.at[0, 0], recv_sem=bsr.at[frm],
            device_id=(frm // halves, 2 * (frm % halves) + core), device_id_type=MESH,
        )

    @pl.loop(1, group)
    def _(k):
        got(k).wait_recv()

    total = lax.fori_loop(
        0, group, lambda k, c: c + br[k].astype(F32), jnp.zeros((2 * cap, sub), F32)
    )
    cg[v] = total.astype(BF16)

    def to_row(k, frm):
        return pltpu.make_async_remote_copy(
            src_ref=cg.at[frm], dst_ref=cg.at[frm], send_sem=cs.at[k], recv_sem=cr.at[frm],
            device_id=(s, (v + k) % n_voc), device_id_type=MESH,
        )

    for k in range(1, n_voc):
        to_row(k, v).start()
    for k in range(1, n_voc):
        to_row(k, (v + n_voc - k) % n_voc).wait_recv()
    per = cap // n_voc
    row_at = lax.broadcasted_iota(jnp.int32, (cap, sub), 0)
    for r in range(per):
        for q in range(n_voc):
            both = cg[q].astype(F32)
            for j in range(2):
                row = jnp.sum(
                    jnp.where(row_at == per * v + r, both[j * cap : (j + 1) * cap], 0.0),
                    axis=0, keepdims=True,
                )
                gh_ref[r : r + 1, q * own_cols + j * sub : q * own_cols + (j + 1) * sub] = row

    picked_out.wait()
    grad_out.wait()
    @pl.loop(1, n_seq)
    def _(k):
        gather1(k, s).wait_send()
        gather2((s + n_seq - k) % n_seq, core).wait_send()
        stats2(k, s).wait_send()

    for k in range(1, n_voc):
        stats1(k, v).wait_send()
        to_row(k, v).wait_send()
    for i in range(halves):
        to_pair(i).wait_send()
        for k in range(1 if i == halves - 1 else 0, n_seq):
            to_owner(i, k).wait_send()


def head_kernel(
    step, g_hbm, p_hbm, gh32_hbm, out_hbm, gh_ref, g_ref, gt_ref, p_ref, gh32_ref, buf, sem, in_sem
):
    taken = [
        pltpu.make_async_copy(src, dst, in_sem.at[i])
        for i, (src, dst) in enumerate(((g_hbm, g_ref), (p_hbm, p_ref), (gh32_hbm, gh32_ref)))
    ]
    for one in taken:
        one.start()
    for one in taken:
        one.wait()
    gh_ref[...] = gh32_ref[...].astype(BF16)
    vocab = g_ref.shape[1]
    full, tail_at, tail = chunks_of(vocab, step)

    def turn(at):
        gt_ref[at, :] = g_ref[:, at].T

    def fill(at):
        buf[at, :] = jnp.dot(gt_ref[at, :], p_ref[...], preferred_element_type=F32).astype(BF16)

    def rows_of(i):
        return pl.ds(pl.multiple_of(i * step, step), step)

    def copy(i):
        rows = pl.ds(pl.multiple_of(i * step, step), step)
        return pltpu.make_async_copy(buf.at[rows], out_hbm.at[rows], sem.at[i])

    def copy_tail():
        if full == 0:
            return pltpu.make_async_copy(buf, out_hbm, sem.at[0])
        rows = pl.ds(tail_at, tail)
        return pltpu.make_async_copy(buf.at[rows], out_hbm.at[rows], sem.at[full])

    if full:
        turn(rows_of(0))

        @pl.loop(0, full - 1)
        def _(i):
            turn(rows_of(i + 1))
            fill(rows_of(i))
            copy(i).start()

    if tail:
        turn(pl.ds(tail_at, tail))
    if full:
        fill(rows_of(full - 1))
        copy(full - 1).start()
    if tail:
        fill(pl.ds(tail_at, tail))
        copy_tail().start()
    if full:
        @pl.loop(0, full)
        def _(i):
            copy(i).wait()
    if tail:
        copy_tail().wait()


def per_device(n_seq, n_voc, hidden, head_weight, teacher, positions, counts):
    slots, vocab = teacher.shape
    depth = hidden.shape[1]
    cap = positions.shape[1]
    halves = n_voc // 2
    group = n_seq * halves
    sub = depth // n_voc // 2
    lanes = -(-slots // 128) * 128
    step = 1024
    n_chunks = chunks_of(vocab, step)[0] + 1
    vmem = pl.BlockSpec(memory_space=pltpu.VMEM)
    smem = pl.BlockSpec(memory_space=pltpu.SMEM)
    anywhere = pl.BlockSpec(memory_space=pl.ANY)
    dma = pltpu.SemaphoreType.DMA
    picked, grad, gh = pl.pallas_call(
        functools.partial(front_kernel, n_seq, n_voc, step),
        out_shape=(
            jax.ShapeDtypeStruct((slots, depth), BF16),
            jax.ShapeDtypeStruct((slots, vocab), BF16),
            jax.ShapeDtypeStruct((cap // n_voc, depth), F32),
        ),
        in_specs=[smem, smem, vmem, vmem, pl.BlockSpec(memory_space=pl.ANY)],
        out_specs=(anywhere, anywhere, vmem),
        scratch_shapes=[
            pltpu.VMEM((vocab, depth), BF16),
            pltpu.VMEM((n_seq, 2, 2 * cap, depth // 4), BF16),
            pltpu.VMEM((slots, depth), BF16),
            pltpu.VMEM((slots, vocab), F32),
            pltpu.VMEM((slots, vocab), F32),
            pltpu.VMEM((slots, vocab), BF16),
            pltpu.VMEM((4 * slots, vocab), BF16),
            pltpu.VMEM((2, n_voc, 2, slots, sub), F32),
            pltpu.VMEM((n_voc, 8, lanes), F32),
            pltpu.VMEM((n_seq, 8, lanes), F32),
            pltpu.VMEM((halves, 2, slots, sub), F32),
            pltpu.VMEM((halves, 2, slots, sub), F32),
            pltpu.VMEM((halves, n_seq, 2 * cap, sub), BF16),
            pltpu.VMEM((group, 2 * cap, sub), BF16),
            pltpu.VMEM((n_voc, 2 * cap, sub), BF16),
            dma((n_chunks,)),
            dma((n_seq,)), dma((n_seq,)), dma((n_seq,)), dma((n_seq,)),
            dma((n_voc,)), dma((n_voc,)), dma((n_seq,)), dma((n_seq,)),
            dma((halves,)), dma((halves,)),
            dma((halves, n_seq)), dma((group,)),
            dma((n_voc,)), dma((n_voc,)), dma((2,)),
        ],
        compiler_params=pltpu.CompilerParams(
            collective_id=0, has_side_effects=True, vmem_limit_bytes=54 * 1024 * 1024
        ),
        cost_estimate=pl.CostEstimate(
            flops=4 * slots * depth * vocab, bytes_accessed=2 * depth * vocab, transcendentals=2 * slots * vocab
        ),
        name="front",
    )(positions, counts, hidden, teacher, head_weight.T)

    rows = 256
    head, gh = pl.pallas_call(
        functools.partial(head_kernel, rows),
        out_shape=(
            jax.ShapeDtypeStruct((vocab, depth), BF16),
            jax.ShapeDtypeStruct((cap // n_voc, depth), BF16),
        ),
        in_specs=[pl.BlockSpec(memory_space=pltpu.HBM)] * 3,
        out_specs=(anywhere, vmem),
        scratch_shapes=[
            pltpu.VMEM((slots, vocab), BF16),
            pltpu.VMEM((vocab, slots), BF16),
            pltpu.VMEM((slots, depth), BF16),
            pltpu.VMEM((cap // n_voc, depth), F32),
            pltpu.VMEM((vocab, depth), BF16),
            dma((chunks_of(vocab, rows)[0] + 1,)),
            dma((3,)),
        ],
        compiler_params=pltpu.CompilerParams(vmem_limit_bytes=60 * 1024 * 1024),
        cost_estimate=pl.CostEstimate(
            flops=2 * slots * depth * vocab, bytes_accessed=2 * depth * vocab, transcendentals=0
        ),
        name="head",
    )(grad, picked, gh)
    return gh, head.T


def solution(mesh):
    return jax.shard_map(
        functools.partial(per_device, mesh.shape["seq"], mesh.shape["vocab"]),
        mesh=mesh,
        in_specs=(
            P("seq", None),
            P(None, ("seq", "vocab")),
            P(None, ("seq", "vocab")),
            P("seq", None),
            P("seq"),
        ),
        out_specs=(P(("seq", "vocab"), None), P(None, ("seq", "vocab"))),
        check_vma=False,
    )
```
